32 devices in a mesh: gx: 4 (over x, core), gy: 4 (over z), gz: 2 (over y).
Axes of the slice: x: 2, y: 2, z: 4, core: 2. Of those that a mesh axis runs over, the one named last changes fastest.
Arguments:
- species: float32 [4, 64, 128, 256], P(None, 'gx', 'gy', 'gz'), may hold values from -6 to 6
- velocity: float32 [3, 64, 128, 256], P(None, 'gx', 'gy', 'gz'), may hold values from -15 to 15
- diffusivity: float32 [64, 128, 256], P('gx', 'gy', 'gz'), may hold values from 0.05 to 1
- reaction: float32 [4, 4], replicated, may hold values from -8 to 8
Outputs:
- updated: float32 [4, 64, 128, 256], P(None, 'gx', 'gy', 'gz')
- gram: float32 [256, 256], P('gx', 'gz')
The draws below stay inside these ranges and needn't reach their ends.
All inputs are finite; a program needn't handle non-finite values. Where the reference program divides by a largest or mean magnitude, that divisor is 1e-20 or more.
Results may differ from the reference program's by a relative error of at most 0.000068.
Values sent between devices are 32-bit elements; how exact they have to be, the bound alone decides.
A program may use at most 64 MiB of HBM per device.

```python
import math
import jax
import jax.numpy as jnp
from jax import lax

NS = 4
NX = 64
NY = 128
NZ = 256


def rolled_ramp(key, length):
    offset = jax.random.randint(key, (), 0, length, dtype=jnp.int32)
    places = (jnp.arange(length, dtype=jnp.int32) + offset) % length
    return places.astype(jnp.float32) / float(length)


def draw_velocity(key, part):
    along_x = rolled_ramp(jax.random.fold_in(key, 11), NX)
    along_y = rolled_ramp(jax.random.fold_in(key, 13), NY)
    along_z = rolled_ramp(jax.random.fold_in(key, 17), NZ)
    grade = 1.0 + 2.0 / 3.0 * (along_x[:, None, None] + along_y[None, :, None] + along_z[None, None, :])
    amplitude = jax.random.uniform(jax.random.fold_in(key, 19), (), jnp.float32, 0.6, 1.0)
    base_key = jax.random.fold_in(key, 23)
    base = jnp.clip(jax.random.normal(base_key, (3, NX, NY, NZ), jnp.float32), -5.0, 5.0)
    return base * (amplitude * grade)[None]


def shard_levels(key, shape, pieces, least, high):
    gain = 1.0
    for dim, blocks in pieces:
        draws = jax.random.uniform(jax.random.fold_in(jax.random.fold_in(key, 6), dim), (blocks,), jnp.float32, least / len(pieces), high / len(pieces))
        gain = gain * jnp.repeat(jnp.exp(draws), shape[dim] // blocks).reshape((-1,) + (1,) * (len(shape) - 1 - dim))
    return gain


def bell_draw(own_key, extent, deviation, limit, shards=(), kind=jnp.bfloat16):
    loudness = shard_levels(own_key, extent, shards, -0.22, 0.18) if shards else 1.0
    entries = jax.random.normal(own_key, extent, jnp.float32) * deviation * loudness
    return jnp.minimum(jnp.maximum(entries, -limit), limit).astype(kind)


def setup_inputs(seed: int = 0) -> dict:
    key_list = jax.random.split(jax.random.key(seed), 5)
    species = bell_draw(key_list[0], (NS, NX, NY, NZ), 1.0, 6.0, ((1, 4), (2, 4), (3, 2)), jnp.float32)
    velocity = draw_velocity(jax.random.fold_in(key_list[4], 71), 0)
    diffusivity = jnp.clip(jnp.exp(math.log(1.0) - 2.9957323 * jax.random.uniform(key_list[2], (NX, NY, NZ), jnp.float32) ** shard_levels(key_list[2], (NX, NY, NZ), ((0, 4), (1, 4), (2, 2)), -0.2, 0.2)), 0.05, 1.0)
    reaction = bell_draw(key_list[3], (NS, NS), 2.0, 8.0, (), jnp.float32)
    return dict(species=species, velocity=velocity, diffusivity=diffusivity, reaction=reaction)


first_coeffs = (4.0 / 5.0, -1.0 / 5.0, 4.0 / 105.0, -1.0 / 280.0)
second_coeffs = (8.0 / 5.0, -1.0 / 5.0, 8.0 / 315.0, -1.0 / 560.0)
centre_weight = -205.0 / 72.0
courant = 0.8


def reference(species, velocity, diffusivity, reaction):
    fastest = jnp.max(jnp.abs(velocity[0]) + jnp.abs(velocity[1]) + jnp.abs(velocity[2]))
    time_step = courant / fastest
    tendency = jnp.einsum("kj,jxyz->kxyz", reaction, species, precision=lax.Precision.HIGHEST)
    for direction in range(3):
        dimension = direction + 1
        first_der = jnp.zeros_like(species)
        second_der = centre_weight * species
        for reach in range(1, 5):
            ahead = jnp.roll(species, -reach, dimension)
            behind = jnp.roll(species, reach, dimension)
            first_der = first_der + first_coeffs[reach - 1] * (ahead - behind)
            second_der = second_der + second_coeffs[reach - 1] * (ahead + behind)
        tendency = tendency - velocity[direction] * first_der + diffusivity * second_der
    updated = species + time_step * tendency
    unfolding = jnp.transpose(updated, (1, 0, 2, 3)).reshape(NX * NS, NY * NZ)
    gram = jnp.dot(unfolding, unfolding.T, precision=lax.Precision.HIGHEST, preferred_element_type=jnp.float32)
    gram = gram / float(NY * NZ)
    return updated, gram
```

```python
import functools

import jax
import jax.numpy as jnp
import numpy as np
from jax import lax
from jax.experimental import pallas as pl
from jax.experimental.pallas import tpu as pltpu
from jax.sharding import PartitionSpec as P

first_coeffs = (4.0 / 5.0, -1.0 / 5.0, 4.0 / 105.0, -1.0 / 280.0)
second_coeffs = (8.0 / 5.0, -1.0 / 5.0, 8.0 / 315.0, -1.0 / 560.0)
centre_weight = -205.0 / 72.0
courant = 0.8
MESH = pl.DeviceIdType.MESH
HIGHEST = lax.Precision.HIGHEST


def lane_matrix(lanes):
    place = np.arange(lanes)
    halo = np.where(place < lanes // 2, place + lanes, place - lanes)
    rows = np.concatenate([place, halo])
    offset = rows[:, None] - place[None, :]
    first = np.zeros(offset.shape)
    second = np.where(offset == 0, 3.0 * centre_weight, 0.0)
    for reach in range(1, 5):
        a, b = first_coeffs[reach - 1], second_coeffs[reach - 1]
        first += a * (offset == reach) - a * (offset == -reach)
        second += b * ((offset == reach) | (offset == -reach))
    return np.concatenate([first, second], axis=1).astype(np.float32)


def kernel(
    sizes, columns_all, sp, vel, dif, reac, lane_mat, out, gram,
    pad, v, d, tend, uout, usend, ufull, zsend, zrecv, msend, mrecv,
    gpart, garecv, gbsend, gbrecv, gcall,
    load_sem, out_sem, own_sem, hs, hr, ms, mr, us, ur, gas, gar, gbs, gbr, gcs, gcr,
):
    count_x, count_y, count_z = sizes
    kinds, nx, ny, lanes = sp.shape
    axes = ("gx", "gy", "gz")
    here = {a: lax.axis_index(a) for a in axes}

    def peer(axis, step):
        n = sizes[axes.index(axis)]
        return {axis: lax.rem(here[axis] + step + n, n)}

    def send(src, dst, s, r, device):
        copy = pltpu.make_async_remote_copy(
            src_ref=src, dst_ref=dst, send_sem=s, recv_sem=r, device_id=device, device_id_type=MESH
        )
        copy.start()
        return copy

    barrier = pltpu.get_barrier_semaphore()
    for axis, n in zip(axes, sizes):
        for step in range(1, n):
            pl.semaphore_signal(barrier, inc=1, device_id=peer(axis, step), device_id_type=MESH)
    loads = [
        pltpu.make_async_copy(vel, v, load_sem.at[0]),
        pltpu.make_async_copy(sp, pad.at[:, 4 : 4 + nx, 8 : 8 + ny, :], load_sem.at[1]),
        pltpu.make_async_copy(dif, d, load_sem.at[2]),
    ]
    for c in loads:
        c.start()
    pl.semaphore_wait(barrier, count_x + count_y + count_z - 3)

    x_halo = [
        send(sp.at[:, nx - 4 :], pad.at[:, 0:4, 8 : 8 + ny, :], hs.at[0], hr.at[0], peer("gx", 1)),
        send(sp.at[:, 0:4], pad.at[:, 4 + nx : 8 + nx, 8 : 8 + ny, :], hs.at[1], hr.at[1], peer("gx", -1)),
    ]
    y_halo = [
        send(sp.at[:, :, ny - 4 :], pad.at[:, 4 : 4 + nx, 4:8, :], hs.at[2], hr.at[2], peer("gy", 1)),
        send(sp.at[:, :, 0:4], pad.at[:, 4 : 4 + nx, 8 + ny : 12 + ny, :], hs.at[3], hr.at[3], peer("gy", -1)),
    ]

    loads[0].wait()

    def speed(x, m):
        s = jnp.abs(v[0, x]) + jnp.abs(v[1, x]) + jnp.abs(v[2, x])
        return jnp.maximum(m, jnp.max(s.reshape(ny // 8, 8, lanes), axis=0))

    most = lax.fori_loop(0, nx, speed, jnp.zeros((8, lanes), jnp.float32))

    def max_start(stage, value):
        n = sizes[stage]
        msend[stage] = value
        return [
            send(msend.at[stage], mrecv.at[stage, k - 1], ms.at[stage, k - 1], mr.at[stage, k - 1], peer(axes[stage], k))
            for k in range(1, n)
        ]

    def max_end(stage, value, copies):
        for k, c in enumerate(copies):
            c.wait()
            value = jnp.maximum(value, mrecv[stage, k])
        return value

    stage_copies = max_start(0, most)

    loads[1].wait()
    lane = lax.broadcasted_iota(jnp.int32, (kinds * ny, lanes), 1)
    edge = (lane < 4) | (lane >= lanes - 4)

    def pack(x, total):
        s = pad[:, 4 + x, 8 : 8 + ny, :].reshape(kinds * ny, lanes)
        return total + pltpu.roll(jnp.where(edge, s, 0.0), 4 + 8 * x, 1)

    zsend[...] = lax.fori_loop(0, nx, pack, jnp.zeros((kinds * ny, lanes), jnp.float32))
    z_halo = [send(zsend, zrecv.at[0], hs.at[4], hr.at[4], peer("gz", 1))]
    if count_z > 2:
        z_halo.append(send(zsend, zrecv.at[1], hs.at[5], hr.at[5], peer("gz", -1)))

    most = max_end(0, most, stage_copies)
    stage_copies = max_start(1, most)

    loads[2].wait()
    for c in z_halo:
        c.wait()
    if count_z > 2:
        wide = lax.broadcasted_iota(jnp.int32, (kinds * ny, lanes), 1) % 8
        zsend[...] = jnp.where(wide < 4, zrecv[0], zrecv[1])
    else:
        zsend[...] = zrecv[0]
    most = max_end(1, most, stage_copies)
    stage_copies = max_start(2, most)
    for c in y_halo:
        c.wait()

    def rest(x, carry):
        s = pad[:, 4 + x, 8 : 8 + ny, :]
        halo = pltpu.roll(zsend[...], lanes - 4 - 8 * x, 1)
        both = jnp.concatenate([s.reshape(kinds * ny, lanes), halo], axis=1)
        along_z = jnp.dot(both, lane_mat[...], precision=HIGHEST, preferred_element_type=jnp.float32)
        z1 = along_z[:, :lanes].reshape(kinds, ny, lanes)
        z2 = along_z[:, lanes:].reshape(kinds, ny, lanes)
        vy, vz, dd = v[1, x], v[2, x], d[x]
        for k in range(kinds):
            first = jnp.zeros((ny, lanes), jnp.float32)
            second = z2[k]
            for r in range(1, 5):
                ahead = pad[k, 4 + x, 8 + r : 8 + ny + r, :]
                behind = pad[k, 4 + x, 8 - r : 8 + ny - r, :]
                first = first + first_coeffs[r - 1] * (ahead - behind)
                second = second + second_coeffs[r - 1] * (ahead + behind)
            t = dd * second - vy * first - vz * z1[k]
            for j in range(kinds):
                t = t + reac[k, j] * s[j]
            tend[k, x] = t
        return carry

    lax.fori_loop(0, nx, rest, 0)

    most = max_end(2, most, stage_copies)
    fastest = jnp.max(most, keepdims=True)
    dt = jnp.broadcast_to(courant / fastest, (ny, lanes))

    share = ny // count_x
    rows_all = count_x * nx * kinds

    def finish(x, carry):
        vx, dd = v[0, x], d[x]
        for k in range(kinds):
            first = jnp.zeros((ny, lanes), jnp.float32)
            second = jnp.zeros((ny, lanes), jnp.float32)
            for r in range(1, 5):
                ahead = pad[k, 4 + x + r, 8 : 8 + ny, :]
                behind = pad[k, 4 + x - r, 8 : 8 + ny, :]
                first = first + first_coeffs[r - 1] * (ahead - behind)
                second = second + second_coeffs[r - 1] * (ahead + behind)
            u = pad[k, 4 + x, 8 : 8 + ny, :] + dt * (tend[k, x] - vx * first + dd * second)
            uout[k, x] = u
            row = pl.multiple_of((x * kinds + k) * share, share)
            usend[:, pl.ds(row, share), :] = u.reshape(count_x, share, lanes)
        return carry

    me_x = here["gx"]
    pending, outs = [], []

    def chunk(index, low, high):
        lax.fori_loop(low, high, finish, 0)
        rows = pl.ds(low * kinds * share, (high - low) * kinds * share)
        start = pl.multiple_of(me_x * (nx * kinds * share) + low * kinds * share, share)
        there = ufull.at[pl.ds(start, (high - low) * kinds * share)]
        for k in range(1, count_x):
            to = peer("gx", k)
            pending.append(
                send(usend.at[to["gx"], rows], there, us.at[index, k - 1], ur.at[index, k - 1], to)
            )
        own = pltpu.make_async_copy(usend.at[me_x, rows], there, own_sem.at[index])
        keep = pltpu.make_async_copy(uout.at[:, low:high], out.at[:, low:high], out_sem.at[index])
        for c in (own, keep):
            c.start()
        pending.append(own)
        outs.append(keep)

    chunk(0, 4, nx - 4)
    x_halo[0].wait()
    chunk(1, 0, 4)
    x_halo[1].wait()
    chunk(2, nx - 4, nx)
    for c in pending:
        c.wait()

    total = jnp.zeros((rows_all, rows_all), jnp.float32)
    for y in range(0, share, 2):
        a = jnp.concatenate([ufull[pl.ds(y + q, rows_all, stride=share), :] for q in range(2)], axis=1)
        total = total + lax.dot_general(
            a, a, (((1,), (1,)), ((), ())), precision=HIGHEST, preferred_element_type=jnp.float32
        )
    rows = nx * kinds
    gpart[...] = total.reshape(count_x, rows, rows_all)
    copies = []
    for k in range(1, count_x):
        to = peer("gx", k)
        copies.append(send(gpart.at[to["gx"]], garecv.at[k - 1], gas.at[k - 1], gar.at[k - 1], to))
    block = gpart[me_x]
    for k, c in enumerate(copies):
        c.wait()
        block = block + garecv[k]
    width = rows_all // count_z
    for k in range(count_z):
        gbsend[k] = block[:, k * width : (k + 1) * width]
    copies = []
    for k in range(1, count_z):
        to = peer("gz", k)
        copies.append(send(gbsend.at[to["gz"]], gbrecv.at[k - 1], gbs.at[k - 1], gbr.at[k - 1], to))
    block = gbsend[here["gz"]]
    for k, c in enumerate(copies):
        c.wait()
        block = block + gbrecv[k]
    me_y = here["gy"]
    gcall[me_y] = block
    copies = [
        send(gcall.at[me_y], gcall.at[me_y], gcs.at[k - 1], gcr.at[k - 1], peer("gy", k)) for k in range(1, count_y)
    ]
    for c in copies:
        c.wait()
    block = gcall[0]
    for k in range(1, count_y):
        block = block + gcall[k]
    gram[...] = block / columns_all
    for c in outs:
        c.wait()


def body(sizes, species, velocity, diffusivity, reaction):
    count_x, count_y, count_z = sizes
    kinds, nx, ny, lanes = species.shape
    rows = nx * kinds
    rows_all = rows * count_x
    width = rows_all // count_z
    columns_all = float(ny * lanes * count_y * count_z)
    most = max(sizes)
    f32 = jnp.float32
    vm = lambda *shape: pltpu.VMEM(shape, f32)
    dma = pltpu.SemaphoreType.DMA
    hbm = pl.BlockSpec(memory_space=pl.ANY)
    vmem = pl.BlockSpec(memory_space=pltpu.VMEM)
    smem = pl.BlockSpec(memory_space=pltpu.SMEM)
    return pl.pallas_call(
        functools.partial(kernel, sizes, columns_all),
        out_shape=(
            jax.ShapeDtypeStruct(species.shape, f32),
            jax.ShapeDtypeStruct((rows, width), f32),
        ),
        in_specs=[hbm, hbm, hbm, smem, vmem],
        out_specs=(hbm, vmem),
        scratch_shapes=[
            vm(kinds, nx + 8, ny + 16, lanes),
            vm(3, nx, ny, lanes),
            vm(nx, ny, lanes),
            vm(kinds, nx, ny, lanes),
            vm(kinds, nx, ny, lanes),
            vm(count_x, rows * ny // count_x, lanes),
            vm(rows * ny, lanes),
            vm(kinds * ny, lanes),
            vm(2, kinds * ny, lanes),
            vm(3, 8, lanes),
            vm(3, most - 1, 8, lanes),
            vm(count_x, rows, rows_all),
            vm(count_x - 1, rows, rows_all),
            vm(count_z, rows, width),
            vm(count_z - 1, rows, width),
            vm(count_y, rows, width),
            dma((3,)), dma((3,)), dma((3,)),
            dma((6,)), dma((6,)),
            dma((3, most - 1)), dma((3, most - 1)),
            dma((3, count_x - 1)), dma((3, count_x - 1)),
            dma((count_x - 1,)), dma((count_x - 1,)),
            dma((count_z - 1,)), dma((count_z - 1,)),
            dma((count_y - 1,)), dma((count_y - 1,)),
        ],
        compiler_params=pltpu.CompilerParams(
            collective_id=0, has_side_effects=True, vmem_limit_bytes=40 * 1024 * 1024
        ),
    )(species, velocity, diffusivity, reaction, jnp.asarray(lane_matrix(lanes)))


def solution(mesh):
    sizes = tuple(mesh.shape[a] for a in ("gx", "gy", "gz"))
    placed = (P(None, "gx", "gy", "gz"), P(None, "gx", "gy", "gz"), P("gx", "gy", "gz"), P())
    return jax.shard_map(
        functools.partial(body, sizes),
        mesh=mesh,
        in_specs=placed,
        out_specs=(P(None, "gx", "gy", "gz"), P("gx", "gz")),
        check_vma=False,
    )
```

```python
import functools

import jax
import jax.numpy as jnp
import numpy as np
from jax import lax
from jax.experimental import pallas as pl
from jax.experimental.pallas import tpu as pltpu
from jax.sharding import PartitionSpec as P

first_coeffs = (4.0 / 5.0, -1.0 / 5.0, 4.0 / 105.0, -1.0 / 280.0)
second_coeffs = (8.0 / 5.0, -1.0 / 5.0, 8.0 / 315.0, -1.0 / 560.0)
centre_weight = -205.0 / 72.0
courant = 0.8
MESH = pl.DeviceIdType.MESH
HIGHEST = lax.Precision.HIGHEST


def lane_matrix(lanes):
    place = np.arange(lanes)
    halo = np.where(place < lanes // 2, place + lanes, place - lanes)
    rows = np.concatenate([place, halo])
    offset = rows[:, None] - place[None, :]
    first = np.zeros(offset.shape)
    second = np.where(offset == 0, 3.0 * centre_weight, 0.0)
    for reach in range(1, 5):
        a, b = first_coeffs[reach - 1], second_coeffs[reach - 1]
        first += a * (offset == reach) - a * (offset == -reach)
        second += b * ((offset == reach) | (offset == -reach))
    return np.concatenate([first, second], axis=1).astype(np.float32)


def kernel(
    sizes, columns_all, sp, vel, dif, reac_in, lane_in, out, gram,
    pad, v, d, reac, lane_mat, tend, uout, usend, ufull, zsend, zrecv, msend, mrecv,
    gpart, garecv, gcall,
    load_sem, out_sem, own_sem, hs, hr, ms, mr, us, ur, gas, gar, gcs, gcr,
):
    count_x, count_y, count_z = sizes
    kinds, nx, ny, lanes = sp.shape
    axes = ("gx", "gy", "gz")
    here = {a: lax.axis_index(a) for a in axes}

    def peer(axis, step):
        n = sizes[axes.index(axis)]
        return {axis: lax.rem(here[axis] + step + n, n)}

    others = [(i, k) for i in range(count_x) for k in range(count_z) if i or k]

    def across(i, k):
        return {"gx": lax.rem(here["gx"] + i, count_x), "gz": lax.rem(here["gz"] + k, count_z)}

    plane = [across(i, k) for i, k in others]
    line = [peer("gy", k) for k in range(1, count_y)]

    def send(src, dst, s, r, device):
        copy = pltpu.make_async_remote_copy(
            src_ref=src, dst_ref=dst, send_sem=s, recv_sem=r, device_id=device, device_id_type=MESH
        )
        copy.start()
        return copy

    barrier = pltpu.get_barrier_semaphore()
    for to in plane + line:
        pl.semaphore_signal(barrier, inc=1, device_id=to, device_id_type=MESH)
    loads = [
        pltpu.make_async_copy(vel, v, load_sem.at[0]),
        pltpu.make_async_copy(sp, pad.at[:, 4 : 4 + nx, 8 : 8 + ny, :], load_sem.at[1]),
        pltpu.make_async_copy(dif, d, load_sem.at[2]),
        pltpu.make_async_copy(reac_in, reac, load_sem.at[3]),
        pltpu.make_async_copy(lane_in, lane_mat, load_sem.at[4]),
    ]
    for c in loads:
        c.start()
    pl.semaphore_wait(barrier, len(plane) + len(line))

    x_halo = [
        send(sp.at[:, nx - 4 :], pad.at[:, 0:4, 8 : 8 + ny, :], hs.at[0], hr.at[0], peer("gx", 1)),
        send(sp.at[:, 0:4], pad.at[:, 4 + nx : 8 + nx, 8 : 8 + ny, :], hs.at[1], hr.at[1], peer("gx", -1)),
    ]
    y_halo = [
        send(sp.at[:, :, ny - 4 :], pad.at[:, 4 : 4 + nx, 4:8, :], hs.at[2], hr.at[2], peer("gy", 1)),
        send(sp.at[:, :, 0:4], pad.at[:, 4 : 4 + nx, 8 + ny : 12 + ny, :], hs.at[3], hr.at[3], peer("gy", -1)),
    ]

    loads[0].wait()

    def speed(x, m):
        s = jnp.abs(v[0, x]) + jnp.abs(v[1, x]) + jnp.abs(v[2, x])
        return jnp.maximum(m, jnp.max(s.reshape(ny // 8, 8, lanes), axis=0))

    most = lax.fori_loop(0, nx, speed, jnp.zeros((8, lanes), jnp.float32))

    def max_start(stage, value):
        msend[stage] = value
        return [
            send(msend.at[stage], mrecv.at[stage, k], ms.at[stage, k], mr.at[stage, k], to)
            for k, to in enumerate((plane, line)[stage])
        ]

    def max_end(stage, value, copies):
        for k, c in enumerate(copies):
            c.wait()
            value = jnp.maximum(value, mrecv[stage, k])
        return value

    stage_copies = max_start(0, most)

    loads[1].wait()
    lane = lax.broadcasted_iota(jnp.int32, (kinds * ny, lanes), 1)
    edge = (lane < 4) | (lane >= lanes - 4)

    def pack(x, total):
        s = pad[:, 4 + x, 8 : 8 + ny, :].reshape(kinds * ny, lanes)
        return total + pltpu.roll(jnp.where(edge, s, 0.0), 4 + 8 * x, 1)

    zsend[...] = lax.fori_loop(0, nx, pack, jnp.zeros((kinds * ny, lanes), jnp.float32))
    z_halo = [send(zsend, zrecv.at[0], hs.at[4], hr.at[4], peer("gz", 1))]
    if count_z > 2:
        z_halo.append(send(zsend, zrecv.at[1], hs.at[5], hr.at[5], peer("gz", -1)))

    for c in loads[2:]:
        c.wait()
    most = max_end(0, most, stage_copies)
    stage_copies = max_start(1, most)

    for c in z_halo:
        c.wait()
    if count_z > 2:
        wide = lax.broadcasted_iota(jnp.int32, (kinds * ny, lanes), 1) % 8
        zsend[...] = jnp.where(wide < 4, zrecv[0], zrecv[1])
    else:
        zsend[...] = zrecv[0]
    for c in y_halo:
        c.wait()

    def rest(x, carry):
        s = pad[:, 4 + x, 8 : 8 + ny, :]
        halo = pltpu.roll(zsend[...], lanes - 4 - 8 * x, 1)
        both = jnp.concatenate([s.reshape(kinds * ny, lanes), halo], axis=1)
        along_z = jnp.dot(both, lane_mat[...], precision=HIGHEST, preferred_element_type=jnp.float32)
        z1 = along_z[:, :lanes].reshape(kinds, ny, lanes)
        z2 = along_z[:, lanes:].reshape(kinds, ny, lanes)
        vy, vz, dd = v[1, x], v[2, x], d[x]
        for k in range(kinds):
            first = jnp.zeros((ny, lanes), jnp.float32)
            second = z2[k]
            for r in range(1, 5):
                ahead = pad[k, 4 + x, 8 + r : 8 + ny + r, :]
                behind = pad[k, 4 + x, 8 - r : 8 + ny - r, :]
                first = first + first_coeffs[r - 1] * (ahead - behind)
                second = second + second_coeffs[r - 1] * (ahead + behind)
            t = dd * second - vy * first - vz * z1[k]
            for j in range(kinds):
                t = t + reac[k, j] * s[j]
            tend[k, x] = t
        return carry

    lax.fori_loop(4, nx - 4, rest, 0)
    most = max_end(1, most, stage_copies)
    fastest = jnp.max(most, keepdims=True)
    dt = jnp.broadcast_to(courant / fastest, (ny, lanes))

    share = ny // count_x
    rows_all = count_x * nx * kinds

    def finish(x, carry):
        vx, dd = v[0, x], d[x]
        for k in range(kinds):
            first = jnp.zeros((ny, lanes), jnp.float32)
            second = jnp.zeros((ny, lanes), jnp.float32)
            for r in range(1, 5):
                ahead = pad[k, 4 + x + r, 8 : 8 + ny, :]
                behind = pad[k, 4 + x - r, 8 : 8 + ny, :]
                first = first + first_coeffs[r - 1] * (ahead - behind)
                second = second + second_coeffs[r - 1] * (ahead + behind)
            u = pad[k, 4 + x, 8 : 8 + ny, :] + dt * (tend[k, x] - vx * first + dd * second)
            uout[k, x] = u
            row = pl.multiple_of((x * kinds + k) * share, share)
            usend[:, pl.ds(row, share), :] = u.reshape(count_x, share, lanes)
        return carry

    me_x = here["gx"]
    pending, outs = [], []

    def chunk(index, low, high):
        lax.fori_loop(low, high, finish, 0)
        rows = pl.ds(low * kinds * share, (high - low) * kinds * share)
        start = pl.multiple_of(me_x * (nx * kinds * share) + low * kinds * share, share)
        there = ufull.at[pl.ds(start, (high - low) * kinds * share)]
        for k in range(1, count_x):
            to = peer("gx", k)
            pending.append(
                send(usend.at[to["gx"], rows], there, us.at[index, k - 1], ur.at[index, k - 1], to)
            )
        own = pltpu.make_async_copy(usend.at[me_x, rows], there, own_sem.at[index])
        keep = pltpu.make_async_copy(uout.at[:, low:high], out.at[:, low:high], out_sem.at[index])
        for c in (own, keep):
            c.start()
        pending.append(own)
        outs.append(keep)

    chunk(0, 4, nx - 4)
    lax.fori_loop(0, 4, rest, 0)
    x_halo[0].wait()
    chunk(1, 0, 4)
    lax.fori_loop(nx - 4, nx, rest, 0)
    x_halo[1].wait()
    chunk(2, nx - 4, nx)
    for c in pending:
        c.wait()

    total = jnp.zeros((rows_all, rows_all), jnp.float32)
    for y in range(0, share, 2):
        a = jnp.concatenate([ufull[pl.ds(y + q, rows_all, stride=share), :] for q in range(2)], axis=1)
        total = total + lax.dot_general(
            a, a, (((1,), (1,)), ((), ())), precision=HIGHEST, preferred_element_type=jnp.float32
        )
    rows = nx * kinds
    width = rows_all // count_z
    for k in range(count_z):
        gpart[:, k] = total[:, k * width : (k + 1) * width].reshape(count_x, rows, width)
    copies = [
        send(gpart.at[to["gx"], to["gz"]], garecv.at[k], gas.at[k], gar.at[k], to) for k, to in enumerate(plane)
    ]
    block = gpart[me_x, here["gz"]]
    for k, c in enumerate(copies):
        c.wait()
        block = block + garecv[k]
    me_y = here["gy"]
    gcall[me_y] = block
    copies = [
        send(gcall.at[me_y], gcall.at[me_y], gcs.at[k], gcr.at[k], to) for k, to in enumerate(line)
    ]
    for c in copies:
        c.wait()
    block = gcall[0]
    for k in range(1, count_y):
        block = block + gcall[k]
    gram[...] = block / columns_all
    for c in outs:
        c.wait()


def place(a, b, out_a, out_b, hold_a, hold_b, sems, sem):
    kinds, nx = a.shape[:2]
    half = nx // 2
    pairs = [
        (
            pltpu.make_async_copy(a.at[k, part], hold_a.at[k, part], sems.at[i]),
            pltpu.make_async_copy(hold_a.at[k, part], out_a.at[k, part], sems.at[2 * kinds + i]),
        )
        for i, (k, part) in enumerate((k, pl.ds(h * half, half)) for k in range(kinds) for h in range(2))
    ]
    pairs.append((pltpu.make_async_copy(b, hold_b, sem.at[0]), pltpu.make_async_copy(hold_b, out_b, sem.at[1])))
    for c, _ in pairs:
        c.start()
    for c, e in pairs:
        c.wait()
        e.start()
    for _, e in pairs:
        e.wait()


def body(sizes, species, velocity, diffusivity, reaction):
    count_x, count_y, count_z = sizes
    kinds, nx, ny, lanes = species.shape
    rows = nx * kinds
    rows_all = rows * count_x
    width = rows_all // count_z
    columns_all = float(ny * lanes * count_y * count_z)
    plane = count_x * count_z - 1
    most = max(plane, count_y - 1)
    f32 = jnp.float32
    vm = lambda *shape: pltpu.VMEM(shape, f32)
    dma = pltpu.SemaphoreType.DMA
    hbm = pl.BlockSpec(memory_space=pl.ANY)
    vmem = pl.BlockSpec(memory_space=pltpu.VMEM)
    got = pl.pallas_call(
        functools.partial(kernel, sizes, columns_all),
        out_shape=(
            jax.ShapeDtypeStruct(species.shape, f32),
            jax.ShapeDtypeStruct((rows, width), f32),
        ),
        in_specs=[hbm] * 5,
        out_specs=(hbm, vmem),
        scratch_shapes=[
            vm(kinds, nx + 8, ny + 16, lanes),
            vm(3, nx, ny, lanes),
            vm(nx, ny, lanes),
            pltpu.SMEM((kinds, kinds), f32),
            vm(2 * lanes, 2 * lanes),
            vm(kinds, nx, ny, lanes),
            vm(kinds, nx, ny, lanes),
            vm(count_x, rows * ny // count_x, lanes),
            vm(rows * ny, lanes),
            vm(kinds * ny, lanes),
            vm(2, kinds * ny, lanes),
            vm(2, 8, lanes),
            vm(2, most, 8, lanes),
            vm(count_x, count_z, rows, width),
            vm(plane, rows, width),
            vm(count_y, rows, width),
            dma((5,)), dma((3,)), dma((3,)),
            dma((6,)), dma((6,)),
            dma((2, most)), dma((2, most)),
            dma((3, count_x - 1)), dma((3, count_x - 1)),
            dma((plane,)), dma((plane,)),
            dma((count_y - 1,)), dma((count_y - 1,)),
        ],
        compiler_params=pltpu.CompilerParams(
            collective_id=0, has_side_effects=True, vmem_limit_bytes=60 * 1024 * 1024
        ),
    )(species, velocity, diffusivity, reaction, jnp.asarray(lane_matrix(lanes)))
    return pl.pallas_call(
        place,
        out_shape=tuple(jax.ShapeDtypeStruct(g.shape, f32) for g in got),
        in_specs=[hbm] * 2,
        out_specs=(hbm, hbm),
        scratch_shapes=[vm(*got[0].shape), vm(*got[1].shape), dma((4 * kinds,)), dma((2,))],
    )(*got)


def solution(mesh):
    sizes = tuple(mesh.shape[a] for a in ("gx", "gy", "gz"))
    placed = (P(None, "gx", "gy", "gz"), P(None, "gx", "gy", "gz"), P("gx", "gy", "gz"), P())
    return jax.shard_map(
        functools.partial(body, sizes),
        mesh=mesh,
        in_specs=placed,
        out_specs=(P(None, "gx", "gy", "gz"), P("gx", "gz")),
        check_vma=False,
    )
```

```python
import functools

import jax
import jax.numpy as jnp
import numpy as np
from jax import lax
from jax.experimental import pallas as pl
from jax.experimental.pallas import tpu as pltpu
from jax.sharding import PartitionSpec as P

first_coeffs = (4.0 / 5.0, -1.0 / 5.0, 4.0 / 105.0, -1.0 / 280.0)
second_coeffs = (8.0 / 5.0, -1.0 / 5.0, 8.0 / 315.0, -1.0 / 560.0)
centre_weight = -205.0 / 72.0
courant = 0.8
MESH = pl.DeviceIdType.MESH
HIGHEST = lax.Precision.HIGHEST


def lane_matrix(lanes):
    place = np.arange(lanes)
    halo = np.where(place < lanes // 2, place + lanes, place - lanes)
    rows = np.concatenate([place, halo])
    offset = rows[:, None] - place[None, :]
    first = np.zeros(offset.shape)
    second = np.where(offset == 0, 3.0 * centre_weight, 0.0)
    for reach in range(1, 5):
        a, b = first_coeffs[reach - 1], second_coeffs[reach - 1]
        first += a * (offset == reach) - a * (offset == -reach)
        second += b * ((offset == reach) | (offset == -reach))
    return np.concatenate([first, second], axis=1).astype(np.float32)


def kernel(
    sizes, columns_all, sp, vel, dif, reac_in, lane_in, out, gram,
    pad, v, d, reac, lane_mat, tend, uout, usend, ufull, zsend, zrecv, msend, mrecv,
    gpart, garecv, gcall,
    load_sem, out_sem, own_sem, hs, hr, ms, mr, us, ur, gas, gar, gcs, gcr,
):
    count_x, count_y, count_z = sizes
    kinds, nx, ny, lanes = sp.shape
    axes = ("gx", "gy", "gz")
    here = {a: lax.axis_index(a) for a in axes}

    def peer(axis, step):
        n = sizes[axes.index(axis)]
        return {axis: lax.rem(here[axis] + step + n, n)}

    others = [(i, k) for i in range(count_x) for k in range(count_z) if i or k]

    def across(i, k):
        return {"gx": lax.rem(here["gx"] + i, count_x), "gz": lax.rem(here["gz"] + k, count_z)}

    plane = [across(i, k) for i, k in others]
    line = [peer("gy", k) for k in range(1, count_y)]

    def send(src, dst, s, r, device):
        copy = pltpu.make_async_remote_copy(
            src_ref=src, dst_ref=dst, send_sem=s, recv_sem=r, device_id=device, device_id_type=MESH
        )
        copy.start()
        return copy

    barrier = pltpu.get_barrier_semaphore()
    for to in plane + line:
        pl.semaphore_signal(barrier, inc=1, device_id=to, device_id_type=MESH)
    loads = [
        *(pltpu.make_async_copy(vel.at[i], v.at[i], load_sem.at[i]) for i in range(3)),
        *(
            pltpu.make_async_copy(sp.at[k], pad.at[k, 4 : 4 + nx, 8 : 8 + ny, :], load_sem.at[5 + k])
            for k in range(kinds)
        ),
        pltpu.make_async_copy(dif, d, load_sem.at[5 + kinds]),
        pltpu.make_async_copy(reac_in, reac, load_sem.at[3]),
        pltpu.make_async_copy(lane_in, lane_mat, load_sem.at[4]),
    ]
    for c in loads:
        c.start()
    pl.semaphore_wait(barrier, len(plane) + len(line))

    x_halo = [
        send(sp.at[:, nx - 4 :], pad.at[:, 0:4, 8 : 8 + ny, :], hs.at[0], hr.at[0], peer("gx", 1)),
        send(sp.at[:, 0:4], pad.at[:, 4 + nx : 8 + nx, 8 : 8 + ny, :], hs.at[1], hr.at[1], peer("gx", -1)),
    ]
    y_halo = [
        send(sp.at[:, :, ny - 4 :], pad.at[:, 4 : 4 + nx, 4:8, :], hs.at[2], hr.at[2], peer("gy", 1)),
        send(sp.at[:, :, 0:4], pad.at[:, 4 : 4 + nx, 8 + ny : 12 + ny, :], hs.at[3], hr.at[3], peer("gy", -1)),
    ]

    for c in loads[:3]:
        c.wait()

    def speed(x, m):
        s = jnp.abs(v[0, x]) + jnp.abs(v[1, x]) + jnp.abs(v[2, x])
        return jnp.maximum(m, jnp.max(s.reshape(ny // 8, 8, lanes), axis=0))

    most = lax.fori_loop(0, nx, speed, jnp.zeros((8, lanes), jnp.float32))

    def max_start(stage, value):
        msend[stage] = value
        return [
            send(msend.at[stage], mrecv.at[stage, k], ms.at[stage, k], mr.at[stage, k], to)
            for k, to in enumerate((plane, line)[stage])
        ]

    def max_end(stage, value, copies):
        for k, c in enumerate(copies):
            c.wait()
            value = jnp.maximum(value, mrecv[stage, k])
        return value

    stage_copies = max_start(0, most)

    for c in loads[3 : 3 + kinds]:
        c.wait()
    lane = lax.broadcasted_iota(jnp.int32, (kinds * ny, lanes), 1)
    edge = (lane < 4) | (lane >= lanes - 4)

    def pack(x, total):
        s = pad[:, 4 + x, 8 : 8 + ny, :].reshape(kinds * ny, lanes)
        return total + pltpu.roll(jnp.where(edge, s, 0.0), 4 + 8 * x, 1)

    zsend[...] = lax.fori_loop(0, nx, pack, jnp.zeros((kinds * ny, lanes), jnp.float32))
    z_halo = [send(zsend, zrecv.at[0], hs.at[4], hr.at[4], peer("gz", 1))]
    if count_z > 2:
        z_halo.append(send(zsend, zrecv.at[1], hs.at[5], hr.at[5], peer("gz", -1)))

    for c in loads[3 + kinds :]:
        c.wait()
    most = max_end(0, most, stage_copies)
    stage_copies = max_start(1, most)

    for c in z_halo:
        c.wait()
    if count_z > 2:
        wide = lax.broadcasted_iota(jnp.int32, (kinds * ny, lanes), 1) % 8
        zsend[...] = jnp.where(wide < 4, zrecv[0], zrecv[1])
    else:
        zsend[...] = zrecv[0]
    for c in y_halo:
        c.wait()

    def rest(x, carry):
        s = pad[:, 4 + x, 8 : 8 + ny, :]
        halo = pltpu.roll(zsend[...], lanes - 4 - 8 * x, 1)
        both = jnp.concatenate([s.reshape(kinds * ny, lanes), halo], axis=1)
        along_z = jnp.dot(both, lane_mat[...], precision=HIGHEST, preferred_element_type=jnp.float32)
        z1 = along_z[:, :lanes].reshape(kinds, ny, lanes)
        z2 = along_z[:, lanes:].reshape(kinds, ny, lanes)
        vy, vz, dd = v[1, x], v[2, x], d[x]
        for k in range(kinds):
            first = jnp.zeros((ny, lanes), jnp.float32)
            second = z2[k]
            for r in range(1, 5):
                ahead = pad[k, 4 + x, 8 + r : 8 + ny + r, :]
                behind = pad[k, 4 + x, 8 - r : 8 + ny - r, :]
                first = first + first_coeffs[r - 1] * (ahead - behind)
                second = second + second_coeffs[r - 1] * (ahead + behind)
            t = dd * second - vy * first - vz * z1[k]
            for j in range(kinds):
                t = t + reac[k, j] * s[j]
            tend[k, x] = t
        return carry

    lax.fori_loop(4, nx - 4, rest, 0)
    most = max_end(1, most, stage_copies)
    fastest = jnp.max(most, keepdims=True)
    dt = jnp.broadcast_to(courant / fastest, (ny, lanes))

    share = ny // count_x
    rows_all = count_x * nx * kinds

    def finish(x, carry):
        vx, dd = v[0, x], d[x]
        for k in range(kinds):
            first = jnp.zeros((ny, lanes), jnp.float32)
            second = jnp.zeros((ny, lanes), jnp.float32)
            for r in range(1, 5):
                ahead = pad[k, 4 + x + r, 8 : 8 + ny, :]
                behind = pad[k, 4 + x - r, 8 : 8 + ny, :]
                first = first + first_coeffs[r - 1] * (ahead - behind)
                second = second + second_coeffs[r - 1] * (ahead + behind)
            u = pad[k, 4 + x, 8 : 8 + ny, :] + dt * (tend[k, x] - vx * first + dd * second)
            uout[k, x] = u
            row = pl.multiple_of((x * kinds + k) * share, share)
            usend[:, pl.ds(row, share), :] = u.reshape(count_x, share, lanes)
        return carry

    me_x = here["gx"]
    pending, outs = [], []

    def chunk(index, low, high):
        lax.fori_loop(low, high, finish, 0)
        rows = pl.ds(low * kinds * share, (high - low) * kinds * share)
        start = pl.multiple_of(me_x * (nx * kinds * share) + low * kinds * share, share)
        there = ufull.at[pl.ds(start, (high - low) * kinds * share)]
        for k in sorted(range(1, count_x), key=lambda k: abs(2 * k - count_x)):
            to = peer("gx", k)
            pending.append(
                send(usend.at[to["gx"], rows], there, us.at[index, k - 1], ur.at[index, k - 1], to)
            )
        own = pltpu.make_async_copy(usend.at[me_x, rows], there, own_sem.at[index])
        keep = pltpu.make_async_copy(uout.at[:, low:high], out.at[:, low:high], out_sem.at[index])
        for c in (own, keep):
            c.start()
        pending.append(own)
        outs.append(keep)

    chunk(0, 4, nx - 4)
    lax.fori_loop(0, 4, rest, 0)
    x_halo[0].wait()
    chunk(1, 0, 4)
    lax.fori_loop(nx - 4, nx, rest, 0)
    x_halo[1].wait()
    chunk(2, nx - 4, nx)
    for c in pending:
        c.wait()

    total = jnp.zeros((rows_all, rows_all), jnp.float32)
    for y in range(0, share, 2):
        a = jnp.concatenate([ufull[pl.ds(y + q, rows_all, stride=share), :] for q in range(2)], axis=1)
        big = a.astype(jnp.bfloat16)
        small = (a - big.astype(jnp.float32)).astype(jnp.bfloat16)
        for left, right in ((big, big), (big, small), (small, big)):
            total = total + lax.dot_general(
                left, right, (((1,), (1,)), ((), ())), preferred_element_type=jnp.float32
            )
    rows = nx * kinds
    width = rows_all // count_z
    for k in range(count_z):
        gpart[:, k] = total[:, k * width : (k + 1) * width].reshape(count_x, rows, width)
    pieces = 2
    size = rows // pieces
    parts = [pl.ds(h * size, size) for h in range(pieces)]
    first_sends = [
        [
            send(gpart.at[to["gx"], to["gz"], part], garecv.at[k, part], gas.at[h, k], gar.at[h, k], to)
            for k, to in enumerate(plane)
        ]
        for h, part in enumerate(parts)
    ]
    me_y, me_z = here["gy"], here["gz"]
    last_sends = []
    for h, part in enumerate(parts):
        block = gpart[me_x, me_z, part]
        for k, c in enumerate(first_sends[h]):
            c.wait()
            block = block + garecv[k, part]
        gcall[me_y, part] = block
        last_sends.append(
            [
                send(gcall.at[me_y, part], gcall.at[me_y, part], gcs.at[h, k], gcr.at[h, k], to)
                for k, to in enumerate(line)
            ]
        )
    for h, part in enumerate(parts):
        for c in last_sends[h]:
            c.wait()
        block = gcall[0, part]
        for k in range(1, count_y):
            block = block + gcall[k, part]
        gram[part] = block / columns_all
    for c in outs:
        c.wait()


def place(a, b, out_a, out_b, hold_a, hold_b, sems, sem):
    kinds, nx = a.shape[:2]
    half = nx // 2
    pairs = [
        (
            pltpu.make_async_copy(a.at[k, part], hold_a.at[k, part], sems.at[i]),
            pltpu.make_async_copy(hold_a.at[k, part], out_a.at[k, part], sems.at[2 * kinds + i]),
        )
        for i, (k, part) in enumerate((k, pl.ds(h * half, half)) for k in range(kinds) for h in range(2))
    ]
    pairs.append((pltpu.make_async_copy(b, hold_b, sem.at[0]), pltpu.make_async_copy(hold_b, out_b, sem.at[1])))
    for c, _ in pairs:
        c.start()
    for c, e in pairs:
        c.wait()
        e.start()
    for _, e in pairs:
        e.wait()


def body(sizes, species, velocity, diffusivity, reaction):
    count_x, count_y, count_z = sizes
    kinds, nx, ny, lanes = species.shape
    rows = nx * kinds
    rows_all = rows * count_x
    width = rows_all // count_z
    columns_all = float(ny * lanes * count_y * count_z)
    plane = count_x * count_z - 1
    most = max(plane, count_y - 1)
    f32 = jnp.float32
    vm = lambda *shape: pltpu.VMEM(shape, f32)
    dma = pltpu.SemaphoreType.DMA
    hbm = pl.BlockSpec(memory_space=pl.ANY)
    vmem = pl.BlockSpec(memory_space=pltpu.VMEM)
    got = pl.pallas_call(
        functools.partial(kernel, sizes, columns_all),
        out_shape=(
            jax.ShapeDtypeStruct(species.shape, f32),
            jax.ShapeDtypeStruct((rows, width), f32),
        ),
        in_specs=[hbm] * 5,
        out_specs=(hbm, vmem),
        scratch_shapes=[
            vm(kinds, nx + 8, ny + 16, lanes),
            vm(3, nx, ny, lanes),
            vm(nx, ny, lanes),
            pltpu.SMEM((kinds, kinds), f32),
            vm(2 * lanes, 2 * lanes),
            vm(kinds, nx, ny, lanes),
            vm(kinds, nx, ny, lanes),
            vm(count_x, rows * ny // count_x, lanes),
            vm(rows * ny, lanes),
            vm(kinds * ny, lanes),
            vm(2, kinds * ny, lanes),
            vm(2, 8, lanes),
            vm(2, most, 8, lanes),
            vm(count_x, count_z, rows, width),
            vm(plane, rows, width),
            vm(count_y, rows, width),
            dma((6 + kinds,)), dma((3,)), dma((3,)),
            dma((6,)), dma((6,)),
            dma((2, most)), dma((2, most)),
            dma((3, count_x - 1)), dma((3, count_x - 1)),
            dma((2, plane)), dma((2, plane)),
            dma((2, count_y - 1)), dma((2, count_y - 1)),
        ],
        compiler_params=pltpu.CompilerParams(
            collective_id=0, has_side_effects=True, vmem_limit_bytes=60 * 1024 * 1024
        ),
    )(species, velocity, diffusivity, reaction, jnp.asarray(lane_matrix(lanes)))
    return pl.pallas_call(
        place,
        out_shape=tuple(jax.ShapeDtypeStruct(g.shape, f32) for g in got),
        in_specs=[hbm] * 2,
        out_specs=(hbm, hbm),
        scratch_shapes=[vm(*got[0].shape), vm(*got[1].shape), dma((4 * kinds,)), dma((2,))],
    )(*got)


def solution(mesh):
    sizes = tuple(mesh.shape[a] for a in ("gx", "gy", "gz"))
    placed = (P(None, "gx", "gy", "gz"), P(None, "gx", "gy", "gz"), P("gx", "gy", "gz"), P())
    return jax.shard_map(
        functools.partial(body, sizes),
        mesh=mesh,
        in_specs=placed,
        out_specs=(P(None, "gx", "gy", "gz"), P("gx", "gz")),
        check_vma=False,
    )
```
